32 devices in a mesh: horiz: 8 (over z, x), depth: 4 (over y, core).
Axes of the slice: x: 2, y: 2, z: 4, core: 2. Of those that a mesh axis runs over, the one named last changes fastest.
Arguments:
- adjoint_seed: bfloat16 [16, 48, 8192], P(None, 'depth', 'horiz'), may hold values from -6 to 6
- transport: bfloat16 [48, 64, 5, 128, 128], P('depth', 'horiz'), may hold values from -0.25 to 0.25
- neighbours: int32 [64, 5], P('horiz'), may hold values from 0 to 63, as said below
- inv_mix: float32 [48, 48, 8192], P(None, None, ('horiz', 'depth')), may hold values from -0.875 to 0.875
- rates: float32 [48, 8192], P('depth', 'horiz'), may hold values from 0.2 to 2
- coupling: float32 [16, 16], replicated, may hold values from -1.5 to 1.5
- sensitivity: bfloat16 [16, 48, 8192], P(None, 'depth', 'horiz')
- depth_count: int32 [8192], P('horiz'), may hold values from 0 to 48, as said below
Outputs:
- first: bfloat16 [16, 48, 8192], P(None, 'depth', 'horiz')
- second: bfloat16 [16, 48, 8192], P(None, 'depth', 'horiz')
- gradient: float32 [16], replicated
The draws below stay inside these ranges and needn't reach their ends.
Inputs may be any that keep to these rules, and one draw needn't show every extreme that they name: neighbours[b, 0] = b; every entry lies within 8 blocks of its row's block b, counted cyclically over 64 blocks. `depth_count`: 0 marks a land column.
All inputs are finite; a program needn't handle non-finite values.
Results may differ from the reference program's by a relative error of at most 0.011.
Values may be sent and summed in bfloat16 or wider, within the bound.
A program may use at most 128 MiB of HBM per device.

```python
import math
import jax
import jax.numpy as jnp
from jax import lax

TR = 16
L = 48
COLBLK = 128
K = 5
BLK_DEV = 8
NBLK = 64
COLS = 8192


def draw_neighbours(key, part):
    key = jax.random.fold_in(key, 11)
    reach = BLK_DEV
    offsets = jax.random.randint(key, (NBLK, K), -reach, reach + 1)
    row_ids = jnp.arange(NBLK, dtype=jnp.int32)
    offsets = offsets.at[:, 0].set(0)
    marked = row_ids % BLK_DEV == 0
    offsets = offsets.at[:, 1].set(jnp.where(marked, reach, offsets[:, 1]))
    offsets = offsets.at[:, 2].set(jnp.where(marked, -reach, offsets[:, 2]))
    return ((row_ids[:, None] + offsets) % NBLK).astype(jnp.int32)


def draw_depth_count(key, part):
    key = jax.random.fold_in(key, 12)
    key_land, key_levels = jax.random.split(key)
    land = jax.random.randint(key_land, (COLS,), 0, 10) < 3
    levels = jax.random.randint(key_levels, (COLS,), 1, L + 1)
    levels = levels.at[1].set(L)
    counts = jnp.where(land, 0, levels)
    counts = counts.at[0].set(0)
    return counts.astype(jnp.int32)


def draw_sensitivity(key, part):
    key = jax.random.fold_in(key, 13)
    key_main = jax.random.fold_in(key, 0)
    position = jnp.arange(COLS, dtype=jnp.float32) / COLS
    growth = (1.0 + 2.0 * position)[None, None, :]
    values = jax.random.normal(key_main, (TR, L, COLS), jnp.float32) * growth
    return values.astype(jnp.bfloat16)


def block_levels(rng, extent, pieces, least, high):
    def one(dim, shards_of):
        steps = jax.random.uniform(jax.random.fold_in(jax.random.fold_in(rng, 6), dim), (shards_of,), jnp.float32, least / len(pieces), high / len(pieces))
        return jnp.repeat(jnp.exp(steps), extent[dim] // shards_of).reshape((-1,) + (1,) * (len(extent) - dim - 1))

    factor_of = one(*pieces[0])
    for cut in pieces[1:]:
        factor_of = factor_of * one(*cut)
    return factor_of


def centred(key, dims, width, most, shards=(), kind=jnp.bfloat16):
    drawn = jax.random.normal(key, dims, jnp.float32) * width
    if len(shards) > 0:
        drawn = block_levels(key, dims, shards, -0.22, 0.18) * drawn
    return jnp.clip(drawn, min=-most, max=most).astype(kind)


def setup_inputs(seed: int = 0) -> dict:
    arg_keys = jax.random.split(jax.random.key(seed), 9)
    return {
        "adjoint_seed": centred(arg_keys[0], (TR, L, COLS), 1.0, 6.0, ((1, 4), (2, 8))),
        "transport": centred(arg_keys[1], (L, NBLK, K, COLBLK, COLBLK), (K * COLBLK) ** -0.5, 0.25, ((0, 4), (1, 8))),
        "neighbours": draw_neighbours(jax.random.fold_in(arg_keys[8], 71), 0),
        "inv_mix": centred(arg_keys[3], (L, L, COLS), L ** -0.5, 0.875, ((2, 32),), jnp.float32),
        "rates": jnp.clip(jnp.exp(math.log(2.0) - 2.3025851 * jax.random.uniform(arg_keys[4], (L, COLS), jnp.float32) ** block_levels(arg_keys[4], (L, COLS), ((0, 4), (1, 8)), -0.2, 0.2)), 0.2, 2.0),
        "coupling": centred(arg_keys[5], (TR, TR), TR ** -0.5, 1.5, (), jnp.float32),
        "sensitivity": draw_sensitivity(jax.random.fold_in(arg_keys[8], 71), 0),
        "depth_count": draw_depth_count(jax.random.fold_in(arg_keys[8], 71), 0),
    }


def reference(adjoint_seed, transport, neighbours, inv_mix, rates, coupling, sensitivity, depth_count):
    level_ids = jnp.arange(L, dtype=jnp.int32)[:, None]
    wet = (level_ids < depth_count[None, :]).astype(jnp.float32)
    state = adjoint_seed
    results = []
    grad_total = jnp.zeros((TR,), jnp.float32)
    sens = sensitivity.astype(jnp.float32)
    for step in range(2):
        mixed = jnp.einsum('pqc,tpc->tqc', inv_mix, state.astype(jnp.float32), precision=lax.Precision.HIGHEST).astype(jnp.bfloat16)
        mixed_f = mixed.astype(jnp.float32)
        by_level = jnp.transpose(mixed.reshape(TR, L, NBLK, COLBLK), (1, 0, 2, 3))

        def level_fn(pair):
            weights, level_vec = pair
            picked = level_vec[:, neighbours]
            return jnp.einsum('bkij,tbkj->tbi', weights.astype(jnp.float32), picked.astype(jnp.float32), precision=lax.Precision.HIGHEST)
        moved = lax.map(level_fn, (transport, by_level))
        moved = jnp.transpose(moved, (1, 0, 2, 3)).reshape(TR, L, COLS)
        source_term = rates[None, :, :] * jnp.einsum('ut,ulc->tlc', coupling, mixed_f, precision=lax.Precision.HIGHEST)
        new_state = (wet[None] * (moved + source_term - state.astype(jnp.float32))).astype(jnp.bfloat16)
        grad_total = grad_total + lax.optimization_barrier(jnp.sum(wet[None] * mixed_f * sens, axis=(1, 2)))
        results.append(new_state)
        state = new_state
    gradient = grad_total / math.sqrt(L * COLS)
    return (results[0], results[1], gradient)
```

```python
import functools
import math

import jax
import jax.numpy as jnp
from jax import lax
from jax.experimental import pallas as pl
from jax.experimental.pallas import tpu as pltpu
from jax.sharding import PartitionSpec as P

CHUNKS = 4
LANES = 128
MESH = pl.DeviceIdType.MESH


def flip(index, stride):
    return index + stride * (1 - 2 * ((index // stride) % 2))


def kernel(nh, nd, dims, *refs):
    tr, lev, blocks, slots = dims
    lc = lev // CHUNKS
    pair = blocks // nd
    pad = -(-lev // 8) * 8
    rounds = [("depth", 1 << i) for i in range(nd.bit_length() - 1)]
    rounds += [("horiz", 1 << i) for i in range(nh.bit_length() - 1)]

    (rows_ref, seed_ref, trans_hbm, inv_hbm, rates_ref, coup_ref, sens_ref, count_ref) = refs[:8]
    first_ref, second_ref, grad_ref = refs[8:11]
    rest = list(refs[11:])
    trans, inv, stage_a, stage_b, senst, zacc, gacc, gsend, grecv = rest[:9]
    vs = rest[9:11]
    vfull = rest[11:13]
    zsend = rest[13:15]
    near = [rest[15 : 15 + CHUNKS], rest[15 + CHUNKS : 15 + 2 * CHUNKS]]
    (tsem, isem, vss, vrs, zss, zrs, pss, prs, fss, frs, gss, grs) = rest[15 + 2 * CHUNKS :]

    h = lax.axis_index("horiz")
    d = lax.axis_index("depth")
    odd = h % 2
    partner = h + 1 - 2 * odd
    ahead = (h + 2 - 4 * odd + nh) % nh
    behind = (h - 2 + 4 * odd + nh) % nh
    seen = 2 * blocks * (1 - odd)
    peers = [(d + k) % nd for k in range(nd)]

    inv_copy = pltpu.make_async_copy(inv_hbm, inv, isem)
    inv_copy.start()
    trans_copies = []
    for c in range(CHUNKS):
        part = pl.ds(c * lc, lc)
        trans_copies.append(pltpu.make_async_copy(trans_hbm.at[part], trans.at[part], tsem.at[c]))
        trans_copies[-1].start()

    barrier = pltpu.get_barrier_semaphore()
    greet = [(h, peers[k]) for k in range(1, nd)] + [(ahead, d), (behind, d)]
    greet += [(flip(h, s), d) for axis, s in rounds if axis == "horiz"]
    for device in greet:
        pl.semaphore_signal(barrier, inc=1, device_id=device, device_id_type=MESH)

    def spread(src, stage):
        def one(t, _):
            row = src[t].astype(jnp.float32)
            for b in range(blocks):
                stage[b, pl.ds(pl.multiple_of(t * pad, 8), lev), :] = row[:, b * LANES : (b + 1) * LANES]
            return 0

        lax.fori_loop(0, tr, one, 0)

    def gather(src, out):
        def one(t, _):
            for b in range(blocks):
                row = src[b, pl.ds(pl.multiple_of(t * pad, 8), lev), :]
                out[t, :, cols(b)] = row.astype(jnp.bfloat16)
            return 0

        lax.fori_loop(0, tr, one, 0)

    def cols(b):
        return pl.ds(b * LANES, LANES)

    def keep_own(a, c):
        part = pl.ds(c * lc, lc)
        vfull[a][d, part] = vs[a][d, part]

    sent = []

    def send_v(a, c):
        part = pl.ds(c * lc, lc)
        keep_own(a, c)
        copies = []
        for k in range(1, nd):
            copy = pltpu.make_async_remote_copy(
                src_ref=vs[a].at[peers[k], part],
                dst_ref=vfull[a].at[d, part],
                send_sem=vss.at[a, c, k - 1],
                recv_sem=vrs.at[a, c, k - 1],
                device_id=(h, peers[k]),
                device_id_type=MESH,
            )
            copy.start()
            copies.append(copy)
        sent.extend(copies)
        return copies

    def mix_rows(a, c, blk, rows, accs):
        def body(i, accs):
            s, j = i // lc, c * lc + i % lc
            v = vfull[a][s, j, blk].astype(jnp.float32)
            return tuple(
                acc + inv[s * lev + j, q : q + 1, cols(blk)] * v for acc, q in zip(accs, rows)
            )

        return lax.fori_loop(0, nd * lc, body, tuple(accs), unroll=True)

    def mix_pass(a, c):
        for g in range(nd):
            for blk in range(pair):
                if c == 0:
                    accs = [jnp.zeros((tr, LANES), jnp.float32)] * lev
                else:
                    accs = [zacc[g, l, blk] for l in range(lev)]
                accs = mix_rows(a, c, blk, range(g * lev, (g + 1) * lev), accs)
                for l, acc in enumerate(accs):
                    zacc[g, l, blk] = acc

    def mix_last(a, z):
        spots = [(g, z * lc + j) for g in range(nd) for j in range(lc)]
        for blk in range(pair):
            accs = [zacc[g, l, blk] for g, l in spots]
            accs = mix_rows(a, CHUNKS - 1, blk, [g * lev + l for g, l in spots], accs)
            for i, acc in enumerate(accs):
                zsend[a][i // lc, z, blk, i % lc] = acc.astype(jnp.bfloat16)
        near[a][z][pl.ds(blocks + pair * d, pair)] = zsend[a][d, z]
        copies = []
        for k in range(1, nd):
            copy = pltpu.make_async_remote_copy(
                src_ref=zsend[a].at[peers[k], z],
                dst_ref=near[a][z].at[pl.ds(blocks + pair * d, pair)],
                send_sem=zss.at[a, z, k - 1],
                recv_sem=zrs.at[a, z, k - 1],
                device_id=(h, peers[k]),
                device_id_type=MESH,
            )
            copy.start()
            copies.append(copy)
        sent.extend(copies)
        return copies

    def wet(l, b):
        return count_ref[:, cols(b)] > d * lev + l

    def to_partner(a, z, back):
        for copy in back:
            copy.wait_recv()
        copy = pltpu.make_async_remote_copy(
            src_ref=near[a][z].at[pl.ds(blocks, blocks)],
            dst_ref=near[a][z].at[pl.ds(2 * blocks - seen, blocks)],
            send_sem=pss.at[a, z],
            recv_sem=prs.at[a, z],
            device_id=(partner, d),
            device_id_type=MESH,
        )
        copy.start()
        sent.append(copy)

        def one(j, g):
            for b in range(blocks):
                l = z * lc + j
                value = near[a][z][blocks + b, j].astype(jnp.float32) * senst[l, b]
                g = g + jnp.where(wet(l, b), value, 0.0)
            return g

        gacc[...] = lax.fori_loop(0, lc, one, gacc[...])
        return copy

    def onward(a, z, arrived):
        arrived.wait_recv()
        copy = pltpu.make_async_remote_copy(
            src_ref=near[a][z].at[pl.ds(seen, blocks)],
            dst_ref=near[a][z].at[pl.ds(2 * blocks - seen, blocks)],
            send_sem=fss.at[a, z],
            recv_sem=frs.at[a, z],
            device_id=(ahead, d),
            device_id_type=MESH,
        )
        copy.start()
        sent.append(copy)
        return copy

    def apply(a, z, arrived):
        arrived.wait_recv()
        stage = (stage_a, stage_b)[a]
        if a == 0:
            trans_copies[z].wait()
        where = [[rows_ref[b, k] for k in range(slots)] for b in range(blocks)]
        coup = coup_ref[...]

        def one(j, _):
            l = z * lc + j
            for b in range(blocks):
                own = near[a][z][blocks + b, j]
                picked = [own] + [near[a][z][where[b][k], j] for k in range(1, slots)]
                moved = lax.dot_general(
                    jnp.concatenate(picked, axis=1),
                    jnp.concatenate([trans[l, b, k] for k in range(slots)], axis=1),
                    (((1,), (1,)), ((), ())),
                    preferred_element_type=jnp.float32,
                )
                source = jnp.dot(
                    coup, jnp.concatenate([own, own], axis=0), preferred_element_type=jnp.float32
                )
                source = rates_ref[l, :, cols(b)] * source
                old = vs[a][b // pair, l, b % pair].astype(jnp.float32)
                new = jnp.where(wet(l, b), moved + source - old, 0.0)
                stage[b, pl.ds(l, tr, stride=pad), :] = new
                if a == 0:
                    vs[1][b // pair, l, b % pair] = new.astype(jnp.bfloat16)
            return 0

        lax.fori_loop(0, lc, one, 0)

    spread(seed_ref, stage_a)
    pl.semaphore_wait(barrier, len(greet))
    v_in = [[], []]
    for c in range(CHUNKS):

        def seed_level(j, _):
            l = c * lc + j
            for b in range(blocks):
                tile = stage_a[b, pl.ds(l, tr, stride=pad), :]
                vs[0][b // pair, l, b % pair] = tile.astype(jnp.bfloat16)
            return 0

        lax.fori_loop(0, lc, seed_level, 0)
        v_in[0].append(send_v(0, c))

    spread(sens_ref, stage_b)

    def sens_level(l, _):
        for b in range(blocks):
            senst[l, b] = stage_b[b, pl.ds(l, tr, stride=pad), :]
        return 0

    lax.fori_loop(0, lev, sens_level, 0)
    gacc[...] = jnp.zeros_like(gacc)
    inv_copy.wait()

    def mix_wait(a, c):
        for copy in v_in[a][c]:
            copy.wait_recv()
        if c < CHUNKS - 1:
            mix_pass(a, c)

    gstate = {"round": 0, "copy": None}

    def grad_step():
        r = gstate["round"]
        if gstate["copy"] is not None:
            gstate["copy"].wait_recv()
            gsend[r] = gsend[r - 1] + grecv[r - 1]
            gstate["copy"] = None
        if r < len(rounds):
            axis, s = rounds[r]
            device = (h, flip(d, s)) if axis == "depth" else (flip(h, s), d)
            copy = pltpu.make_async_remote_copy(
                src_ref=gsend.at[r],
                dst_ref=grecv.at[r],
                send_sem=gss.at[r],
                recv_sem=grs.at[r],
                device_id=device,
                device_id_type=MESH,
            )
            copy.start()
            sent.append(copy)
            gstate["copy"] = copy
            gstate["round"] = r + 1

    for c in range(CHUNKS - 1):
        mix_wait(0, c)
    for a in range(2):
        mix_wait(a, CHUNKS - 1)
        back = [mix_last(a, z) for z in range(CHUNKS)]
        if a == 1:
            gather(stage_a, first_ref)
        crossing, forward = [], []

        def finish(z):
            apply(a, z, forward[z])
            if a == 0:
                v_in[1].append(send_v(1, z))
                if z > 0:
                    mix_wait(1, z - 1)

        for z in range(CHUNKS):
            while len(crossing) < min(CHUNKS, z + 2):
                crossing.append(to_partner(a, len(crossing), back[len(crossing)]))
            forward.append(onward(a, z, crossing[z]))
            if z + 2 < CHUNKS:
                crossing.append(to_partner(a, z + 2, back[z + 2]))
            if a == 1 and len(crossing) == CHUNKS:
                if gstate["round"] == 0:
                    gsend[0] = gacc[...]
                grad_step()
            if z > 0:
                finish(z - 1)
        if a == 1:
            grad_step()
        finish(CHUNKS - 1)
    gather(stage_b, second_ref)
    while gstate["copy"] is not None:
        grad_step()
    total = jnp.sum(gsend[len(rounds)], axis=1, keepdims=True)
    scale = math.sqrt(lev * nd * blocks * nh * LANES)
    grad_ref[...] = jnp.broadcast_to(total / scale, (tr, LANES))
    for copy in sent:
        copy.wait_send()


def per_device(nh, nd, seed, transport, neighbours, inv_mix, rates, coupling, sensitivity, count):
    tr, lev, _ = seed.shape
    blocks, slots = neighbours.shape
    lc = lev // CHUNKS
    pair = blocks // nd
    pad = -(-lev // 8) * 8
    n_rounds = nd.bit_length() + nh.bit_length() - 2
    ids = lax.axis_index("horiz") * blocks + jnp.arange(blocks, dtype=jnp.int32)
    steps = (neighbours - ids[:, None] + blocks) % (blocks * nh)
    rows = jnp.arange(blocks, dtype=jnp.int32)[:, None] + steps
    high = coupling.T.astype(jnp.bfloat16)
    low = (coupling.T - high.astype(jnp.float32)).astype(jnp.bfloat16)
    coup = jnp.concatenate([high, low], axis=1)
    bf16, f32 = jnp.bfloat16, jnp.float32
    vmem = pl.BlockSpec(memory_space=pltpu.VMEM)
    hbm = pl.BlockSpec(memory_space=pltpu.HBM)
    tile = (tr, LANES)
    dma = pltpu.SemaphoreType.DMA
    vsem = dma((2, CHUNKS, nd - 1))
    zsem = dma((2, CHUNKS))
    first, second, grad = pl.pallas_call(
        functools.partial(kernel, nh, nd, (tr, lev, blocks, slots)),
        out_shape=(
            jax.ShapeDtypeStruct(seed.shape, bf16),
            jax.ShapeDtypeStruct(seed.shape, bf16),
            jax.ShapeDtypeStruct(tile, f32),
        ),
        in_specs=[
            pl.BlockSpec(memory_space=pltpu.SMEM), vmem, hbm, hbm, vmem, vmem, vmem, vmem,
        ],
        out_specs=(vmem, vmem, vmem),
        scratch_shapes=[
            pltpu.VMEM(transport.shape, bf16),
            pltpu.VMEM(inv_mix.shape, f32),
            pltpu.VMEM((blocks, tr * pad, LANES), f32),
            pltpu.VMEM((blocks, tr * pad, LANES), f32),
            pltpu.VMEM((lev, blocks) + tile, f32),
            pltpu.VMEM((nd, lev, pair) + tile, f32),
            pltpu.VMEM(tile, f32),
            pltpu.VMEM((n_rounds + 1,) + tile, f32),
            pltpu.VMEM((n_rounds,) + tile, f32),
        ]
        + [pltpu.VMEM((nd, lev, pair) + tile, bf16)] * 4
        + [pltpu.VMEM((nd, CHUNKS, pair, lc) + tile, bf16)] * 2
        + [pltpu.VMEM((3 * blocks, lc) + tile, bf16)] * (2 * CHUNKS)
        + [dma((CHUNKS,)), dma]
        + [vsem, vsem, vsem, vsem, zsem, zsem, zsem, zsem, dma((n_rounds,)), dma((n_rounds,))],
        compiler_params=pltpu.CompilerParams(
            collective_id=0, has_side_effects=True, vmem_limit_bytes=44 * 1024 * 1024
        ),
        cost_estimate=pl.CostEstimate(
            flops=4 * transport.size * tr, bytes_accessed=2 * transport.size, transcendentals=0
        ),
    )(rows, seed, transport, inv_mix, rates[:, None, :], coup, sensitivity, count[None, :])
    return first, second, grad[:, 0]


def solution(mesh):
    return jax.shard_map(
        functools.partial(per_device, mesh.shape["horiz"], mesh.shape["depth"]),
        mesh=mesh,
        in_specs=(
            P(None, "depth", "horiz"),
            P("depth", "horiz", None, None, None),
            P("horiz", None),
            P(None, None, ("horiz", "depth")),
            P("depth", "horiz"),
            P(),
            P(None, "depth", "horiz"),
            P("horiz"),
        ),
        out_specs=(P(None, "depth", "horiz"), P(None, "depth", "horiz"), P()),
        check_vma=False,
    )
```

```python
import functools
import math

import jax
import jax.numpy as jnp
from jax import lax
from jax.experimental import pallas as pl
from jax.experimental.pallas import tpu as pltpu
from jax.sharding import PartitionSpec as P

CHUNKS = 4
LANES = 128
MESH = pl.DeviceIdType.MESH
NT = (((1,), (1,)), ((), ()))


def flip(index, stride):
    return index + stride * (1 - 2 * ((index // stride) % 2))


def kernel(nh, nd, dims, *refs):
    tr, lev, blocks, slots = dims
    lc = lev // CHUNKS
    pair = blocks // nd
    rounds = [("depth", 1 << i) for i in range(nd.bit_length() - 1)]
    rounds += [("horiz", 1 << i) for i in range(nh.bit_length() - 1)]

    near_ref, seed_hbm, trans_hbm, inv_hbm, rates_hbm, coup_hbm, sens_hbm, count_hbm = refs[:8]
    first_ref, second_ref, grad_ref = refs[8:11]
    rest = list(refs[11:])
    trans, inv, rates, rate_rows, coup_in, coup_ref, sens, count = rest[:8]
    part_h, zacc, gacc, gsend, grecv = rest[8:13]
    vs = rest[13:15]
    vfull = rest[15:17]
    zsend = rest[17:19]
    near = [rest[19 : 19 + CHUNKS], rest[19 + CHUNKS : 19 + 2 * CHUNKS]]
    (ssem, tsem, isem, vss, vrs, zss, zrs, pss, prs, fss, frs, gss, grs) = rest[19 + 2 * CHUNKS :]

    h = lax.axis_index("horiz")
    d = lax.axis_index("depth")
    odd = h % 2
    partner = h + 1 - 2 * odd
    ahead = (h + 2 - 4 * odd + nh) % nh
    behind = (h - 2 + 4 * odd + nh) % nh
    seen = 2 * blocks * (1 - odd)
    peers = [(d + k) % nd for k in range(nd)]

    def cols(b):
        return pl.ds(b * LANES, LANES)

    def load(src, dst, sem):
        copy = pltpu.make_async_copy(src, dst, sem)
        copy.start()
        return copy

    seed_copies = [
        load(seed_hbm.at[:, :, cols(b)], vs[0].at[b // pair, :, b % pair], ssem.at[b])
        for b in range(blocks)
    ]
    inv_copy = load(inv_hbm, inv, isem.at[0])
    small_copies = [
        load(src, dst, isem.at[i + 1])
        for i, (src, dst) in enumerate(
            [(rates_hbm, rates), (coup_hbm, coup_in), (sens_hbm, sens), (count_hbm, count)]
        )
    ]
    trans_copies = []
    for c in range(CHUNKS):
        part = pl.ds(c * lc, lc)
        trans_copies.append(load(trans_hbm.at[part], trans.at[part], tsem.at[c]))
    where = [
        [near_ref[b, k] for k in range(slots)] for b in range(blocks)
    ]

    barrier = pltpu.get_barrier_semaphore()
    greet = [(h, peers[k]) for k in range(1, nd)] + [(ahead, d), (behind, d)]
    greet += [(flip(h, s), d) for axis, s in rounds if axis == "horiz"]
    for device in greet:
        pl.semaphore_signal(barrier, inc=1, device_id=device, device_id_type=MESH)

    def keep_own(a, c):
        part = pl.ds(c * lc, lc)
        vfull[a][d, part] = vs[a][d, part]

    sent = []

    def send_v(a, c):
        part = pl.ds(c * lc, lc)
        keep_own(a, c)
        copies = []
        for k in range(1, nd):
            copy = pltpu.make_async_remote_copy(
                src_ref=vs[a].at[peers[k], part],
                dst_ref=vfull[a].at[d, part],
                send_sem=vss.at[a, c, k - 1],
                recv_sem=vrs.at[a, c, k - 1],
                device_id=(h, peers[k]),
                device_id_type=MESH,
            )
            copy.start()
            copies.append(copy)
        sent.extend(copies)
        return copies

    def mix_rows(a, c, blk, rows, accs):
        def body(i, accs):
            s, j = i // lc, c * lc + i % lc
            v = vfull[a][s, j, blk].astype(jnp.float32)
            return tuple(
                acc + inv[s * lev + j, q : q + 1, cols(blk)] * v for acc, q in zip(accs, rows)
            )

        return lax.fori_loop(0, nd * lc, body, tuple(accs), unroll=True)

    def mix_pass(a, c):
        for g in range(nd):
            for blk in range(pair):
                if c == 0:
                    accs = [jnp.zeros((tr, LANES), jnp.float32)] * lev
                else:
                    accs = [zacc[g, l, blk] for l in range(lev)]
                accs = mix_rows(a, c, blk, range(g * lev, (g + 1) * lev), accs)
                for l, acc in enumerate(accs):
                    zacc[g, l, blk] = acc

    def mix_last(a, z):
        spots = [(g, z * lc + j) for g in range(nd) for j in range(lc)]
        for blk in range(pair):
            accs = [zacc[g, l, blk] for g, l in spots]
            accs = mix_rows(a, CHUNKS - 1, blk, [g * lev + l for g, l in spots], accs)
            for i, acc in enumerate(accs):
                zsend[a][i // lc, z, blk, i % lc] = acc.astype(jnp.bfloat16)
        near[a][z][pl.ds(blocks + pair * d, pair)] = zsend[a][d, z]
        copies = []
        for k in range(1, nd):
            copy = pltpu.make_async_remote_copy(
                src_ref=zsend[a].at[peers[k], z],
                dst_ref=near[a][z].at[pl.ds(blocks + pair * d, pair)],
                send_sem=zss.at[a, z, k - 1],
                recv_sem=zrs.at[a, z, k - 1],
                device_id=(h, peers[k]),
                device_id_type=MESH,
            )
            copy.start()
            copies.append(copy)
        sent.extend(copies)
        return copies

    def wet(l, b):
        return count[:, cols(b)] > d * lev + l

    def to_partner(a, z, back):
        for copy in back:
            copy.wait_recv()
        copy = pltpu.make_async_remote_copy(
            src_ref=near[a][z].at[pl.ds(blocks, blocks)],
            dst_ref=near[a][z].at[pl.ds(2 * blocks - seen, blocks)],
            send_sem=pss.at[a, z],
            recv_sem=prs.at[a, z],
            device_id=(partner, d),
            device_id_type=MESH,
        )
        copy.start()
        sent.append(copy)

        def one(j, g):
            for b in range(blocks):
                l = z * lc + j
                grade = sens[l, :, cols(b)].astype(jnp.float32)
                value = near[a][z][blocks + b, j].astype(jnp.float32) * grade
                g = g + jnp.where(wet(l, b), value, 0.0)
            return g

        gacc[...] = lax.fori_loop(0, lc, one, gacc[...])
        return copy

    def onward(a, z, arrived):
        arrived.wait_recv()
        copy = pltpu.make_async_remote_copy(
            src_ref=near[a][z].at[pl.ds(seen, blocks)],
            dst_ref=near[a][z].at[pl.ds(2 * blocks - seen, blocks)],
            send_sem=fss.at[a, z],
            recv_sem=frs.at[a, z],
            device_id=(ahead, d),
            device_id_type=MESH,
        )
        copy.start()
        sent.append(copy)
        return copy

    def begin(a, z):
        if a == 0:
            trans_copies[z].wait()
        coup = coup_ref[...]

        def one(j, _):
            l = z * lc + j
            for b in range(blocks):
                own = near[a][z][blocks + b, j]
                moved = lax.dot_general(
                    own, trans[l, b, 0], NT, preferred_element_type=jnp.float32
                )
                source = jnp.dot(
                    coup, jnp.concatenate([own, own], axis=0), preferred_element_type=jnp.float32
                )
                source = rate_rows[l, :, cols(b)] * source
                old = vs[a][b // pair, l, b % pair].astype(jnp.float32)
                part_h[l, b] = moved + source - old
            return 0

        lax.fori_loop(0, lc, one, 0)

    def apply(a, z, arrived):
        arrived.wait_recv()
        out = (first_ref, second_ref)[a]

        def one(j, _):
            l = z * lc + j
            for b in range(blocks):
                picked = [near[a][z][where[b][k], j] for k in range(1, slots)]
                moved = lax.dot_general(
                    jnp.concatenate(picked, axis=1),
                    jnp.concatenate([trans[l, b, k] for k in range(1, slots)], axis=1),
                    NT,
                    preferred_element_type=jnp.float32,
                )
                new = jnp.where(wet(l, b), moved + part_h[l, b], 0.0).astype(jnp.bfloat16)
                out[l, :, cols(b)] = new
                if a == 0:
                    vs[1][b // pair, l, b % pair] = new
            return 0

        lax.fori_loop(0, lc, one, 0)

    for copy in seed_copies:
        copy.wait()
    pl.semaphore_wait(barrier, len(greet))
    v_in = [[], []]
    for c in range(CHUNKS):
        v_in[0].append(send_v(0, c))
    gacc[...] = jnp.zeros_like(gacc)
    for copy in small_copies:
        copy.wait()
    for l in range(lev):
        rate_rows[l] = rates[l : l + 1, :]
    high = coup_in[...].astype(jnp.bfloat16)
    low = (coup_in[...] - high.astype(jnp.float32)).astype(jnp.bfloat16)
    unit = lax.broadcasted_iota(jnp.int32, (tr, tr), 0) == lax.broadcasted_iota(
        jnp.int32, (tr, tr), 1
    )
    unit = unit.astype(jnp.float32).astype(jnp.bfloat16)
    turned = [
        lax.dot_general(unit, x, NT, preferred_element_type=jnp.float32).astype(jnp.bfloat16)
        for x in (high, low)
    ]
    coup_ref[...] = jnp.concatenate(turned, axis=1)
    inv_copy.wait()

    def mix_wait(a, c):
        for copy in v_in[a][c]:
            copy.wait_recv()
        if c < CHUNKS - 1:
            mix_pass(a, c)

    gstate = {"round": 0, "copy": None}

    def grad_step():
        r = gstate["round"]
        if gstate["copy"] is not None:
            gstate["copy"].wait_recv()
            gsend[r] = gsend[r - 1] + grecv[r - 1]
            gstate["copy"] = None
        if r < len(rounds):
            axis, s = rounds[r]
            device = (h, flip(d, s)) if axis == "depth" else (flip(h, s), d)
            copy = pltpu.make_async_remote_copy(
                src_ref=gsend.at[r],
                dst_ref=grecv.at[r],
                send_sem=gss.at[r],
                recv_sem=grs.at[r],
                device_id=device,
                device_id_type=MESH,
            )
            copy.start()
            sent.append(copy)
            gstate["copy"] = copy
            gstate["round"] = r + 1

    for c in range(CHUNKS - 1):
        mix_wait(0, c)
    for a in range(2):
        mix_wait(a, CHUNKS - 1)
        back = [mix_last(a, z) for z in range(CHUNKS)]
        crossing, forward = [], []

        def finish(z):
            apply(a, z, forward[z])
            if a == 0:
                v_in[1].append(send_v(1, z))
                if z > 0:
                    mix_wait(1, z - 1)

        def cross():
            z = len(crossing)
            if z < CHUNKS:
                crossing.append(to_partner(a, z, back[z]))
                begin(a, z)
                if a == 1 and z == CHUNKS - 1:
                    gsend[0] = gacc[...]
                    grad_step()

        cross()
        for z in range(CHUNKS):
            if z == 0:
                cross()
            if a == 1 and z > 1:
                grad_step()
            forward.append(onward(a, z, crossing[z]))
            cross()
            if z > 0:
                finish(z - 1)
                if a == 1 and gstate["round"] > 0:
                    grad_step()
        finish(CHUNKS - 1)
    while gstate["copy"] is not None:
        grad_step()
    summed = jnp.sum(gsend[len(rounds)], axis=1, keepdims=True)
    scale = math.sqrt(lev * nd * blocks * nh * LANES)
    summed = jnp.broadcast_to(summed / scale, (tr, LANES))
    diagonal = lax.broadcasted_iota(jnp.int32, (tr, LANES), 0) == lax.broadcasted_iota(
        jnp.int32, (tr, LANES), 1
    )
    grad_ref[...] = jnp.sum(jnp.where(diagonal, summed, 0.0), axis=0, keepdims=True)
    for copy in sent:
        copy.wait_send()


def per_device(nh, nd, seed, transport, neighbours, inv_mix, rates, coupling, sensitivity, count):
    tr, lev, _ = seed.shape
    blocks, slots = neighbours.shape
    lc = lev // CHUNKS
    pair = blocks // nd
    n_rounds = nd.bit_length() + nh.bit_length() - 2
    ids = lax.axis_index("horiz") * blocks + jnp.arange(blocks, dtype=jnp.int32)
    steps = (neighbours - ids[:, None] + blocks) % (blocks * nh)
    rows = jnp.arange(blocks, dtype=jnp.int32)[:, None] + steps
    seed, sensitivity = (x.transpose(1, 0, 2) for x in (seed, sensitivity))
    bf16, f32 = jnp.bfloat16, jnp.float32
    vmem = pl.BlockSpec(memory_space=pltpu.VMEM)
    hbm = pl.BlockSpec(memory_space=pltpu.HBM)
    tile = (tr, LANES)
    dma = pltpu.SemaphoreType.DMA
    vsem = dma((2, CHUNKS, nd - 1))
    zsem = dma((2, CHUNKS))
    first, second, grad = pl.pallas_call(
        functools.partial(kernel, nh, nd, (tr, lev, blocks, slots)),
        out_shape=(
            jax.ShapeDtypeStruct(seed.shape, bf16),
            jax.ShapeDtypeStruct(seed.shape, bf16),
            jax.ShapeDtypeStruct((1, LANES), f32),
        ),
        in_specs=[
            pl.BlockSpec(memory_space=pltpu.SMEM), hbm, hbm, hbm, hbm, hbm, hbm, hbm,
        ],
        out_specs=(vmem, vmem, vmem),
        scratch_shapes=[
            pltpu.VMEM(transport.shape, bf16),
            pltpu.VMEM(inv_mix.shape, f32),
            pltpu.VMEM(rates.shape, f32),
            pltpu.VMEM((lev, 1, blocks * LANES), f32),
            pltpu.VMEM(coupling.shape, f32),
            pltpu.VMEM((tr, 2 * tr), bf16),
            pltpu.VMEM(sensitivity.shape, bf16),
            pltpu.VMEM((1, blocks * LANES), jnp.int32),
            pltpu.VMEM((lev, blocks) + tile, f32),
            pltpu.VMEM((nd, lev, pair) + tile, f32),
            pltpu.VMEM(tile, f32),
            pltpu.VMEM((n_rounds + 1,) + tile, f32),
            pltpu.VMEM((n_rounds,) + tile, f32),
        ]
        + [pltpu.VMEM((nd, lev, pair) + tile, bf16)] * 4
        + [pltpu.VMEM((nd, CHUNKS, pair, lc) + tile, bf16)] * 2
        + [pltpu.VMEM((3 * blocks, lc) + tile, bf16)] * (2 * CHUNKS)
        + [dma((blocks,)), dma((CHUNKS,)), dma((5,))]
        + [vsem, vsem, vsem, vsem, zsem, zsem, zsem, zsem, dma((n_rounds,)), dma((n_rounds,))],
        compiler_params=pltpu.CompilerParams(
            collective_id=0, has_side_effects=True, vmem_limit_bytes=60 * 1024 * 1024
        ),
        cost_estimate=pl.CostEstimate(
            flops=4 * transport.size * tr, bytes_accessed=2 * transport.size, transcendentals=0
        ),
    )(rows, seed, transport, inv_mix, rates, coupling, sensitivity, count[None, :])
    return first.transpose(1, 0, 2), second.transpose(1, 0, 2), grad[0, :tr]


def solution(mesh):
    return jax.shard_map(
        functools.partial(per_device, mesh.shape["horiz"], mesh.shape["depth"]),
        mesh=mesh,
        in_specs=(
            P(None, "depth", "horiz"),
            P("depth", "horiz", None, None, None),
            P("horiz", None),
            P(None, None, ("horiz", "depth")),
            P("depth", "horiz"),
            P(),
            P(None, "depth", "horiz"),
            P("horiz"),
        ),
        out_specs=(P(None, "depth", "horiz"), P(None, "depth", "horiz"), P()),
        check_vma=False,
    )
```

```python
import functools
import math

import jax
import jax.numpy as jnp
from jax import lax
from jax.experimental import pallas as pl
from jax.experimental.pallas import tpu as pltpu
from jax.sharding import PartitionSpec as P

CHUNKS = 6
LANES = 128
MESH = pl.DeviceIdType.MESH
NT = (((1,), (1,)), ((), ()))


def flip(index, stride):
    return index + stride * (1 - 2 * ((index // stride) % 2))


def kernel(nh, nd, dims, *refs):
    tr, lev, blocks, slots = dims
    lc = lev // CHUNKS
    pair = blocks // nd
    rounds = [("depth", 1 << i) for i in range(nd.bit_length() - 1)]
    rounds += [("horiz", 1 << i) for i in range(nh.bit_length() - 1)]

    near_ref, seed_hbm, trans_hbm, inv_hbm, rates_hbm, coup_hbm, sens_hbm, count_hbm = refs[:8]
    first_ref, second_ref, grad_ref = refs[8:11]
    rest = list(refs[11:])
    trans, inv, rates, rate_rows, coup_in, coup_ref, sens, count = rest[:8]
    part_h, zacc, gacc, gsend, grecv = rest[8:13]
    vs = rest[13:15]
    vfull = rest[15:17]
    zsend = rest[17:19]
    near = [rest[19 : 19 + CHUNKS], rest[19 + CHUNKS : 19 + 2 * CHUNKS]]
    (ssem, tsem, isem, vss, vrs, zss, zrs, pss, prs, fss, frs, gss, grs) = rest[19 + 2 * CHUNKS :]

    h = lax.axis_index("horiz")
    d = lax.axis_index("depth")
    odd = h % 2
    partner = h + 1 - 2 * odd
    ahead = (h + 2 - 4 * odd + nh) % nh
    behind = (h - 2 + 4 * odd + nh) % nh
    seen = 2 * blocks * (1 - odd)
    total = blocks * nh
    peers = [(d + k) % nd for k in range(nd)]

    def cols(b):
        return pl.ds(b * LANES, LANES)

    def load(src, dst, sem):
        copy = pltpu.make_async_copy(src, dst, sem)
        copy.start()
        return copy

    seed_copies = [
        load(seed_hbm.at[:, :, cols(b)], vs[0].at[b // pair, :, b % pair], ssem.at[b])
        for b in range(blocks)
    ]
    inv_copy = load(inv_hbm, inv, isem.at[0])
    small_copies = [
        load(src, dst, isem.at[i + 1])
        for i, (src, dst) in enumerate(
            [(rates_hbm, rates), (coup_hbm, coup_in), (sens_hbm, sens), (count_hbm, count)]
        )
    ]
    trans_copies = []
    for c in range(CHUNKS):
        part = pl.ds(c * lc, lc)
        trans_copies.append(load(trans_hbm.at[part], trans.at[part], tsem.at[c]))
    where = [
        [
            b + jnp.minimum((near_ref[b, k] - (h * blocks + b) + blocks + total) % total, 2 * blocks)
            for k in range(slots)
        ]
        for b in range(blocks)
    ]

    barrier = pltpu.get_barrier_semaphore()
    greet = [(h, peers[k]) for k in range(1, nd)] + [(ahead, d), (behind, d)]
    greet += [(flip(h, s), d) for axis, s in rounds if axis == "horiz"]
    for device in greet:
        pl.semaphore_signal(barrier, inc=1, device_id=device, device_id_type=MESH)

    def keep_own(a, c):
        part = pl.ds(c * lc, lc)
        vfull[a][d, part] = vs[a][d, part]

    sent = []

    def send_v(a, c):
        part = pl.ds(c * lc, lc)
        keep_own(a, c)
        copies = []
        for k in range(1, nd):
            copy = pltpu.make_async_remote_copy(
                src_ref=vs[a].at[peers[k], part],
                dst_ref=vfull[a].at[d, part],
                send_sem=vss.at[a, c, k - 1],
                recv_sem=vrs.at[a, c, k - 1],
                device_id=(h, peers[k]),
                device_id_type=MESH,
            )
            copy.start()
            copies.append(copy)
        sent.extend(copies)
        return copies

    def mix_rows(a, c, blk, rows, accs):
        def body(i, accs):
            s, j = i // lc, c * lc + i % lc
            v = vfull[a][s, j, blk].astype(jnp.float32)
            return tuple(
                acc + inv[s * lev + j, q : q + 1, cols(blk)] * v for acc, q in zip(accs, rows)
            )

        return lax.fori_loop(0, nd * lc, body, tuple(accs), unroll=True)

    def mix_pass(a, c):
        for g in range(nd):
            for blk in range(pair):
                if c == 0:
                    accs = [jnp.zeros((tr, LANES), jnp.float32)] * lev
                else:
                    accs = [zacc[g, l, blk] for l in range(lev)]
                accs = mix_rows(a, c, blk, range(g * lev, (g + 1) * lev), accs)
                for l, acc in enumerate(accs):
                    zacc[g, l, blk] = acc

    def mix_last(a, z):
        spots = [(g, z * lc + j) for g in range(nd) for j in range(lc)]
        for blk in range(pair):
            accs = [zacc[g, l, blk] for g, l in spots]
            accs = mix_rows(a, CHUNKS - 1, blk, [g * lev + l for g, l in spots], accs)
            for i, acc in enumerate(accs):
                zsend[a][i // lc, z, blk, i % lc] = acc.astype(jnp.bfloat16)
        near[a][z][pl.ds(blocks + pair * d, pair)] = zsend[a][d, z]
        copies = []
        for k in range(1, nd):
            copy = pltpu.make_async_remote_copy(
                src_ref=zsend[a].at[peers[k], z],
                dst_ref=near[a][z].at[pl.ds(blocks + pair * d, pair)],
                send_sem=zss.at[a, z, k - 1],
                recv_sem=zrs.at[a, z, k - 1],
                device_id=(h, peers[k]),
                device_id_type=MESH,
            )
            copy.start()
            copies.append(copy)
        sent.extend(copies)
        return copies

    def wet(l, b):
        return count[:, cols(b)] > d * lev + l

    def to_partner(a, z, back):
        for copy in back:
            copy.wait_recv()
        copy = pltpu.make_async_remote_copy(
            src_ref=near[a][z].at[pl.ds(blocks, blocks)],
            dst_ref=near[a][z].at[pl.ds(2 * blocks - seen, blocks)],
            send_sem=pss.at[a, z],
            recv_sem=prs.at[a, z],
            device_id=(partner, d),
            device_id_type=MESH,
        )
        copy.start()
        sent.append(copy)

        def one(j, g):
            for b in range(blocks):
                l = z * lc + j
                grade = sens[l, :, cols(b)].astype(jnp.float32)
                value = near[a][z][blocks + b, j].astype(jnp.float32) * grade
                g = g + jnp.where(wet(l, b), value, 0.0)
            return g

        gacc[...] = lax.fori_loop(0, lc, one, gacc[...])
        return copy

    def onward(a, z, arrived):
        arrived.wait_recv()
        copy = pltpu.make_async_remote_copy(
            src_ref=near[a][z].at[pl.ds(seen, blocks)],
            dst_ref=near[a][z].at[pl.ds(2 * blocks - seen, blocks)],
            send_sem=fss.at[a, z],
            recv_sem=frs.at[a, z],
            device_id=(ahead, d),
            device_id_type=MESH,
        )
        copy.start()
        sent.append(copy)
        return copy

    def begin(a, z):
        if a == 0:
            trans_copies[z].wait()
        coup = coup_ref[...]

        def one(j, _):
            l = z * lc + j
            for b in range(blocks):
                own = near[a][z][blocks + b, j]
                moved = lax.dot_general(
                    own, trans[l, b, 0], NT, preferred_element_type=jnp.float32
                )
                source = jnp.dot(
                    coup, jnp.concatenate([own, own], axis=0), preferred_element_type=jnp.float32
                )
                source = rate_rows[l, :, cols(b)] * source
                old = vs[a][b // pair, l, b % pair].astype(jnp.float32)
                part_h[l, b] = moved + source - old
            return 0

        lax.fori_loop(0, lc, one, 0)

    def apply(a, z, arrived):
        arrived.wait_recv()
        out = (first_ref, second_ref)[a]

        def one(j, _):
            l = z * lc + j
            for b in range(blocks):
                picked = [near[a][z][where[b][k], j] for k in range(1, slots)]
                moved = lax.dot_general(
                    jnp.concatenate(picked, axis=1),
                    jnp.concatenate([trans[l, b, k] for k in range(1, slots)], axis=1),
                    NT,
                    preferred_element_type=jnp.float32,
                )
                new = jnp.where(wet(l, b), moved + part_h[l, b], 0.0).astype(jnp.bfloat16)
                out[l, :, cols(b)] = new
                if a == 0:
                    vs[1][b // pair, l, b % pair] = new
            return 0

        lax.fori_loop(0, lc, one, 0)

    for copy in seed_copies:
        copy.wait()
    pl.semaphore_wait(barrier, len(greet))
    v_in = [[], []]
    for c in range(CHUNKS):
        v_in[0].append(send_v(0, c))
    gacc[...] = jnp.zeros_like(gacc)
    for copy in small_copies:
        copy.wait()
    for l in range(lev):
        rate_rows[l] = rates[l : l + 1, :]
    high = coup_in[...].astype(jnp.bfloat16)
    low = (coup_in[...] - high.astype(jnp.float32)).astype(jnp.bfloat16)
    unit = lax.broadcasted_iota(jnp.int32, (tr, tr), 0) == lax.broadcasted_iota(
        jnp.int32, (tr, tr), 1
    )
    unit = unit.astype(jnp.float32).astype(jnp.bfloat16)
    turned = [
        lax.dot_general(unit, x, NT, preferred_element_type=jnp.float32).astype(jnp.bfloat16)
        for x in (high, low)
    ]
    coup_ref[...] = jnp.concatenate(turned, axis=1)
    inv_copy.wait()

    def mix_wait(a, c):
        for copy in v_in[a][c]:
            copy.wait_recv()
        if c < CHUNKS - 1:
            mix_pass(a, c)

    gstate = {"round": 0, "copy": None}

    def grad_step():
        r = gstate["round"]
        if gstate["copy"] is not None:
            gstate["copy"].wait_recv()
            gsend[r] = gsend[r - 1] + grecv[r - 1]
            gstate["copy"] = None
        if r < len(rounds):
            axis, s = rounds[r]
            device = (h, flip(d, s)) if axis == "depth" else (flip(h, s), d)
            copy = pltpu.make_async_remote_copy(
                src_ref=gsend.at[r],
                dst_ref=grecv.at[r],
                send_sem=gss.at[r],
                recv_sem=grs.at[r],
                device_id=device,
                device_id_type=MESH,
            )
            copy.start()
            sent.append(copy)
            gstate["copy"] = copy
            gstate["round"] = r + 1

    for c in range(CHUNKS - 1):
        mix_wait(0, c)
    for a in range(2):
        mix_wait(a, CHUNKS - 1)
        back = [mix_last(a, z) for z in range(CHUNKS)]
        crossing, forward = [], []

        def finish(z):
            apply(a, z, forward[z])
            if a == 0:
                v_in[1].append(send_v(1, z))
                if z > 0:
                    mix_wait(1, z - 1)

        def cross():
            z = len(crossing)
            if z < CHUNKS:
                crossing.append(to_partner(a, z, back[z]))
                begin(a, z)
                if a == 1 and z == CHUNKS - 1:
                    gsend[0] = gacc[...]
                    grad_step()

        cross()
        for z in range(CHUNKS):
            if z == 0:
                cross()
            if a == 1 and gstate["round"] > 0:
                grad_step()
            forward.append(onward(a, z, crossing[z]))
            cross()
            if z > 0:
                finish(z - 1)
                if a == 1 and gstate["round"] > 0:
                    grad_step()
        finish(CHUNKS - 1)
    while gstate["copy"] is not None:
        grad_step()
    summed = jnp.sum(gsend[len(rounds)], axis=1, keepdims=True)
    scale = math.sqrt(lev * nd * blocks * nh * LANES)
    summed = jnp.broadcast_to(summed / scale, (tr, tr))
    diagonal = lax.broadcasted_iota(jnp.int32, (tr, tr), 0) == lax.broadcasted_iota(
        jnp.int32, (tr, tr), 1
    )
    grad_ref[...] = jnp.sum(jnp.where(diagonal, summed, 0.0), axis=0, keepdims=True)
    for copy in sent:
        copy.wait_send()


def hand_out(*refs):
    copies = [pltpu.make_async_copy(refs[i], refs[3 + i], refs[6].at[i]) for i in range(3)]
    for copy in copies:
        copy.start()
    for copy in copies:
        copy.wait()


def per_device(nh, nd, seed, transport, neighbours, inv_mix, rates, coupling, sensitivity, count):
    tr, lev, _ = seed.shape
    blocks, slots = neighbours.shape
    lc = lev // CHUNKS
    pair = blocks // nd
    n_rounds = nd.bit_length() + nh.bit_length() - 2
    seed, sensitivity = (x.transpose(1, 0, 2) for x in (seed, sensitivity))
    bf16, f32 = jnp.bfloat16, jnp.float32
    vmem = pl.BlockSpec(memory_space=pltpu.VMEM)
    hbm = pl.BlockSpec(memory_space=pltpu.HBM)
    tile = (tr, LANES)
    dma = pltpu.SemaphoreType.DMA
    vsem = dma((2, CHUNKS, nd - 1))
    zsem = dma((2, CHUNKS))
    first, second, grad = pl.pallas_call(
        functools.partial(kernel, nh, nd, (tr, lev, blocks, slots)),
        out_shape=(
            jax.ShapeDtypeStruct(seed.shape, bf16),
            jax.ShapeDtypeStruct(seed.shape, bf16),
            jax.ShapeDtypeStruct((1, tr), f32),
        ),
        in_specs=[
            pl.BlockSpec(memory_space=pltpu.SMEM), hbm, hbm, hbm, hbm, hbm, hbm, hbm,
        ],
        out_specs=(vmem, vmem, vmem),
        scratch_shapes=[
            pltpu.VMEM(transport.shape, bf16),
            pltpu.VMEM(inv_mix.shape, f32),
            pltpu.VMEM(rates.shape, f32),
            pltpu.VMEM((lev, 1, blocks * LANES), f32),
            pltpu.VMEM(coupling.shape, f32),
            pltpu.VMEM((tr, 2 * tr), bf16),
            pltpu.VMEM(sensitivity.shape, bf16),
            pltpu.VMEM((1, blocks * LANES), jnp.int32),
            pltpu.VMEM((lev, blocks) + tile, f32),
            pltpu.VMEM((nd, lev, pair) + tile, f32),
            pltpu.VMEM(tile, f32),
            pltpu.VMEM((n_rounds + 1,) + tile, f32),
            pltpu.VMEM((n_rounds,) + tile, f32),
        ]
        + [pltpu.VMEM((nd, lev, pair) + tile, bf16)] * 4
        + [pltpu.VMEM((nd, CHUNKS, pair, lc) + tile, bf16)] * 2
        + [pltpu.VMEM((3 * blocks, lc) + tile, bf16)] * (2 * CHUNKS)
        + [dma((blocks,)), dma((CHUNKS,)), dma((5,))]
        + [vsem, vsem, vsem, vsem, zsem, zsem, zsem, zsem, dma((n_rounds,)), dma((n_rounds,))],
        compiler_params=pltpu.CompilerParams(
            collective_id=0, has_side_effects=True, vmem_limit_bytes=60 * 1024 * 1024
        ),
        cost_estimate=pl.CostEstimate(
            flops=4 * transport.size * tr, bytes_accessed=2 * transport.size, transcendentals=0
        ),
    )(neighbours, seed, transport, inv_mix, rates, coupling, sensitivity, count[None, :])
    results = (first, second, grad)
    first, second, grad = pl.pallas_call(
        hand_out,
        out_shape=tuple(jax.ShapeDtypeStruct(x.shape, x.dtype) for x in results),
        in_specs=[hbm] * 3,
        out_specs=(hbm,) * 3,
        scratch_shapes=[dma((3,))],
        compiler_params=pltpu.CompilerParams(vmem_limit_bytes=60 * 1024 * 1024),
    )(*results)
    return first.transpose(1, 0, 2), second.transpose(1, 0, 2), grad[0]


def solution(mesh):
    return jax.shard_map(
        functools.partial(per_device, mesh.shape["horiz"], mesh.shape["depth"]),
        mesh=mesh,
        in_specs=(
            P(None, "depth", "horiz"),
            P("depth", "horiz", None, None, None),
            P("horiz", None),
            P(None, None, ("horiz", "depth")),
            P("depth", "horiz"),
            P(),
            P(None, "depth", "horiz"),
            P("horiz"),
        ),
        out_specs=(P(None, "depth", "horiz"), P(None, "depth", "horiz"), P()),
        check_vma=False,
    )
```

```python
import functools
import math

import jax
import jax.numpy as jnp
from jax import lax
from jax.experimental import pallas as pl
from jax.experimental.pallas import tpu as pltpu
from jax.sharding import PartitionSpec as P

CHUNKS = 3
LANES = 128
MESH = pl.DeviceIdType.MESH
NT = (((1,), (1,)), ((), ()))


def flip(index, stride):
    return index + stride * (1 - 2 * ((index // stride) % 2))


def kernel(nh, nd, dims, *refs):
    tr, lev, blocks, slots = dims
    lc = lev // CHUNKS
    pair = blocks // nd
    rounds = [("depth", 1 << i) for i in range(nd.bit_length() - 1)]
    rounds += [("horiz", 1 << i) for i in range(nh.bit_length() - 1)]

    near_ref, seed_hbm, trans_hbm, inv_hbm, rates_hbm, coup_hbm, sens_hbm, count_hbm = refs[:8]
    first_ref, second_ref, grad_ref = refs[8:11]
    rest = list(refs[11:])
    trans, inv, rates, rate_rows, coup_in, coup_ref, sens, count = rest[:8]
    part_h, zacc, gacc, gsend, grecv = rest[8:13]
    vs = rest[13:15]
    vfull = rest[15:17]
    zsend = rest[17:19]
    near = [rest[19 : 19 + CHUNKS], rest[19 + CHUNKS : 19 + 2 * CHUNKS]]
    (ssem, tsem, isem, vss, vrs, zss, zrs, pss, prs, fss, frs, gss, grs) = rest[19 + 2 * CHUNKS :]

    h = lax.axis_index("horiz")
    d = lax.axis_index("depth")
    odd = h % 2
    partner = h + 1 - 2 * odd
    ahead = (h + 2 - 4 * odd + nh) % nh
    behind = (h - 2 + 4 * odd + nh) % nh
    seen = 2 * blocks * (1 - odd)
    total = blocks * nh
    peers = [(d + k) % nd for k in range(nd)]

    def cols(b):
        return pl.ds(b * LANES, LANES)

    def load(src, dst, sem):
        copy = pltpu.make_async_copy(src, dst, sem)
        copy.start()
        return copy

    seed_copies = [
        load(seed_hbm.at[:, :, cols(b)], vs[0].at[b // pair, :, b % pair], ssem.at[b])
        for b in range(blocks)
    ]
    inv_copy = load(inv_hbm, inv, isem.at[0])
    small_copies = [
        load(src, dst, isem.at[i + 1])
        for i, (src, dst) in enumerate(
            [(rates_hbm, rates), (coup_hbm, coup_in), (sens_hbm, sens), (count_hbm, count)]
        )
    ]
    trans_copies = []
    for c in range(CHUNKS):
        part = pl.ds(c * lc, lc)
        trans_copies.append(load(trans_hbm.at[part], trans.at[part], tsem.at[c]))
    where = [
        [
            b + jnp.minimum((near_ref[b, k] - (h * blocks + b) + blocks + total) % total, 2 * blocks)
            for k in range(slots)
        ]
        for b in range(blocks)
    ]

    barrier = pltpu.get_barrier_semaphore()
    greet = [(h, peers[k]) for k in range(1, nd)] + [(ahead, d), (behind, d)]
    greet += [(flip(h, s), d) for axis, s in rounds if axis == "horiz"]
    for device in greet:
        pl.semaphore_signal(barrier, inc=1, device_id=device, device_id_type=MESH)

    def keep_own(a, c):
        part = pl.ds(c * lc, lc)
        vfull[a][d, part] = vs[a][d, part]

    sent = []

    def send_v(a, c):
        part = pl.ds(c * lc, lc)
        keep_own(a, c)
        copies = []
        for k in range(1, nd):
            copy = pltpu.make_async_remote_copy(
                src_ref=vs[a].at[peers[k], part],
                dst_ref=vfull[a].at[d, part],
                send_sem=vss.at[a, c, k - 1],
                recv_sem=vrs.at[a, c, k - 1],
                device_id=(h, peers[k]),
                device_id_type=MESH,
            )
            copy.start()
            copies.append(copy)
        sent.extend(copies)
        return copies

    def mix_rows(a, c, blk, rows, accs):
        def body(i, accs):
            s, j = i // lc, c * lc + i % lc
            v = vfull[a][s, j, blk].astype(jnp.float32)
            return tuple(
                acc + inv[s * lev + j, q : q + 1, cols(blk)] * v for acc, q in zip(accs, rows)
            )

        return lax.fori_loop(0, nd * lc, body, tuple(accs), unroll=True)

    def mix_pass(a, c):
        for g in range(nd):
            for blk in range(pair):
                if c == 0:
                    accs = [jnp.zeros((tr, LANES), jnp.float32)] * lev
                else:
                    accs = [zacc[g, l, blk] for l in range(lev)]
                accs = mix_rows(a, c, blk, range(g * lev, (g + 1) * lev), accs)
                for l, acc in enumerate(accs):
                    zacc[g, l, blk] = acc

    def mix_last(a, z):
        spots = [(g, z * lc + j) for g in range(nd) for j in range(lc)]
        for blk in range(pair):
            accs = [zacc[g, l, blk] for g, l in spots]
            accs = mix_rows(a, CHUNKS - 1, blk, [g * lev + l for g, l in spots], accs)
            for i, acc in enumerate(accs):
                zsend[a][i // lc, z, blk, i % lc] = acc.astype(jnp.bfloat16)
        near[a][z][pl.ds(blocks + pair * d, pair)] = zsend[a][d, z]
        copies = []
        for k in range(1, nd):
            copy = pltpu.make_async_remote_copy(
                src_ref=zsend[a].at[peers[k], z],
                dst_ref=near[a][z].at[pl.ds(blocks + pair * d, pair)],
                send_sem=zss.at[a, z, k - 1],
                recv_sem=zrs.at[a, z, k - 1],
                device_id=(h, peers[k]),
                device_id_type=MESH,
            )
            copy.start()
            copies.append(copy)
        sent.extend(copies)
        return copies

    def wet(l, b):
        return count[:, cols(b)] > d * lev + l

    def to_partner(a, z, back):
        for copy in back:
            copy.wait_recv()
        copy = pltpu.make_async_remote_copy(
            src_ref=near[a][z].at[pl.ds(blocks, blocks)],
            dst_ref=near[a][z].at[pl.ds(2 * blocks - seen, blocks)],
            send_sem=pss.at[a, z],
            recv_sem=prs.at[a, z],
            device_id=(partner, d),
            device_id_type=MESH,
        )
        copy.start()
        sent.append(copy)

        def one(j, g):
            for b in range(blocks):
                l = z * lc + j
                grade = sens[l, :, cols(b)].astype(jnp.float32)
                value = near[a][z][blocks + b, j].astype(jnp.float32) * grade
                g = g + jnp.where(wet(l, b), value, 0.0)
            return g

        gacc[...] = lax.fori_loop(0, lc, one, gacc[...])
        return copy

    def onward(a, z, arrived):
        arrived.wait_recv()
        copy = pltpu.make_async_remote_copy(
            src_ref=near[a][z].at[pl.ds(seen, blocks)],
            dst_ref=near[a][z].at[pl.ds(2 * blocks - seen, blocks)],
            send_sem=fss.at[a, z],
            recv_sem=frs.at[a, z],
            device_id=(ahead, d),
            device_id_type=MESH,
        )
        copy.start()
        sent.append(copy)
        return copy

    def begin(a, z):
        if a == 0:
            trans_copies[z].wait()
        coup = coup_ref[...]

        def one(j, _):
            l = z * lc + j
            for b in range(blocks):
                own = near[a][z][blocks + b, j]
                moved = lax.dot_general(
                    own, trans[l, b, 0], NT, preferred_element_type=jnp.float32
                )
                source = jnp.dot(
                    coup, jnp.concatenate([own, own], axis=0), preferred_element_type=jnp.float32
                )
                source = rate_rows[l, :, cols(b)] * source
                old = vs[a][b // pair, l, b % pair].astype(jnp.float32)
                part_h[l, b] = moved + source - old
            return 0

        lax.fori_loop(0, lc, one, 0)

    def apply(a, z, arrived):
        arrived.wait_recv()
        out = (first_ref, second_ref)[a]

        def one(j, _):
            l = z * lc + j
            for b in range(blocks):
                picked = [near[a][z][where[b][k], j] for k in range(1, slots)]
                moved = lax.dot_general(
                    jnp.concatenate(picked, axis=1),
                    jnp.concatenate([trans[l, b, k] for k in range(1, slots)], axis=1),
                    NT,
                    preferred_element_type=jnp.float32,
                )
                new = jnp.where(wet(l, b), moved + part_h[l, b], 0.0).astype(jnp.bfloat16)
                out[l, :, cols(b)] = new
                if a == 0:
                    vs[1][b // pair, l, b % pair] = new
            return 0

        lax.fori_loop(0, lc, one, 0)

    for copy in seed_copies:
        copy.wait()
    pl.semaphore_wait(barrier, len(greet))
    v_in = [[], []]
    for c in range(CHUNKS):
        v_in[0].append(send_v(0, c))
    gacc[...] = jnp.zeros_like(gacc)
    for copy in small_copies:
        copy.wait()
    for l in range(lev):
        rate_rows[l] = rates[l : l + 1, :]
    high = coup_in[...].astype(jnp.bfloat16)
    low = (coup_in[...] - high.astype(jnp.float32)).astype(jnp.bfloat16)
    unit = lax.broadcasted_iota(jnp.int32, (tr, tr), 0) == lax.broadcasted_iota(
        jnp.int32, (tr, tr), 1
    )
    unit = unit.astype(jnp.float32).astype(jnp.bfloat16)
    turned = [
        lax.dot_general(unit, x, NT, preferred_element_type=jnp.float32).astype(jnp.bfloat16)
        for x in (high, low)
    ]
    coup_ref[...] = jnp.concatenate(turned, axis=1)
    inv_copy.wait()

    def mix_wait(a, c):
        for copy in v_in[a][c]:
            copy.wait_recv()
        if c < CHUNKS - 1:
            mix_pass(a, c)

    gstate = {"round": 0, "copy": None}

    def grad_step():
        r = gstate["round"]
        if gstate["copy"] is not None:
            gstate["copy"].wait_recv()
            gsend[r] = gsend[r - 1] + grecv[r - 1]
            gstate["copy"] = None
        if r < len(rounds):
            axis, s = rounds[r]
            device = (h, flip(d, s)) if axis == "depth" else (flip(h, s), d)
            copy = pltpu.make_async_remote_copy(
                src_ref=gsend.at[r],
                dst_ref=grecv.at[r],
                send_sem=gss.at[r],
                recv_sem=grs.at[r],
                device_id=device,
                device_id_type=MESH,
            )
            copy.start()
            sent.append(copy)
            gstate["copy"] = copy
            gstate["round"] = r + 1

    for c in range(CHUNKS - 1):
        mix_wait(0, c)
    for a in range(2):
        mix_wait(a, CHUNKS - 1)
        back = [mix_last(a, z) for z in range(CHUNKS)]
        crossing, forward = [], []

        def finish(z):
            apply(a, z, forward[z])
            if a == 0:
                v_in[1].append(send_v(1, z))
                if z > 0:
                    mix_wait(1, z - 1)

        def cross():
            z = len(crossing)
            if z < CHUNKS:
                crossing.append(to_partner(a, z, back[z]))
                begin(a, z)
                if a == 1 and z == CHUNKS - 1:
                    gsend[0] = gacc[...]
                    grad_step()

        cross()
        for z in range(CHUNKS):
            if z == 0:
                cross()
            if a == 1 and gstate["round"] > 0:
                grad_step()
            forward.append(onward(a, z, crossing[z]))
            cross()
            if z > 0:
                finish(z - 1)
                if a == 1 and gstate["round"] > 0:
                    grad_step()
        finish(CHUNKS - 1)
    while gstate["copy"] is not None:
        grad_step()
    summed = jnp.sum(gsend[len(rounds)], axis=1, keepdims=True)
    scale = math.sqrt(lev * nd * blocks * nh * LANES)
    summed = jnp.broadcast_to(summed / scale, (tr, tr))
    diagonal = lax.broadcasted_iota(jnp.int32, (tr, tr), 0) == lax.broadcasted_iota(
        jnp.int32, (tr, tr), 1
    )
    grad_ref[...] = jnp.sum(jnp.where(diagonal, summed, 0.0), axis=0, keepdims=True)
    for copy in sent:
        copy.wait_send()


def per_device(nh, nd, seed, transport, neighbours, inv_mix, rates, coupling, sensitivity, count):
    tr, lev, _ = seed.shape
    blocks, slots = neighbours.shape
    lc = lev // CHUNKS
    pair = blocks // nd
    n_rounds = nd.bit_length() + nh.bit_length() - 2
    seed, sensitivity = (x.transpose(1, 0, 2) for x in (seed, sensitivity))
    bf16, f32 = jnp.bfloat16, jnp.float32
    vmem = pl.BlockSpec(memory_space=pltpu.VMEM)
    hbm = pl.BlockSpec(memory_space=pltpu.HBM)
    tile = (tr, LANES)
    dma = pltpu.SemaphoreType.DMA
    vsem = dma((2, CHUNKS, nd - 1))
    zsem = dma((2, CHUNKS))
    first, second, grad = pl.pallas_call(
        functools.partial(kernel, nh, nd, (tr, lev, blocks, slots)),
        out_shape=(
            jax.ShapeDtypeStruct(seed.shape, bf16),
            jax.ShapeDtypeStruct(seed.shape, bf16),
            jax.ShapeDtypeStruct((1, tr), f32),
        ),
        in_specs=[
            pl.BlockSpec(memory_space=pltpu.SMEM), hbm, hbm, hbm, hbm, hbm, hbm, hbm,
        ],
        out_specs=(vmem, vmem, vmem),
        scratch_shapes=[
            pltpu.VMEM(transport.shape, bf16),
            pltpu.VMEM(inv_mix.shape, f32),
            pltpu.VMEM(rates.shape, f32),
            pltpu.VMEM((lev, 1, blocks * LANES), f32),
            pltpu.VMEM(coupling.shape, f32),
            pltpu.VMEM((tr, 2 * tr), bf16),
            pltpu.VMEM(sensitivity.shape, bf16),
            pltpu.VMEM((1, blocks * LANES), jnp.int32),
            pltpu.VMEM((lev, blocks) + tile, f32),
            pltpu.VMEM((nd, lev, pair) + tile, f32),
            pltpu.VMEM(tile, f32),
            pltpu.VMEM((n_rounds + 1,) + tile, f32),
            pltpu.VMEM((n_rounds,) + tile, f32),
        ]
        + [pltpu.VMEM((nd, lev, pair) + tile, bf16)] * 4
        + [pltpu.VMEM((nd, CHUNKS, pair, lc) + tile, bf16)] * 2
        + [pltpu.VMEM((3 * blocks, lc) + tile, bf16)] * (2 * CHUNKS)
        + [dma((blocks,)), dma((CHUNKS,)), dma((5,))]
        + [vsem, vsem, vsem, vsem, zsem, zsem, zsem, zsem, dma((n_rounds,)), dma((n_rounds,))],
        compiler_params=pltpu.CompilerParams(
            collective_id=0, has_side_effects=True, vmem_limit_bytes=60 * 1024 * 1024
        ),
        cost_estimate=pl.CostEstimate(
            flops=4 * transport.size * tr, bytes_accessed=2 * transport.size, transcendentals=0
        ),
    )(neighbours, seed, transport, inv_mix, rates, coupling, sensitivity, count[None, :])
    first, second = (x.transpose(1, 0, 2) for x in (first, second))
    level_ids = lax.broadcasted_iota(jnp.int32, first.shape, 1) + lax.axis_index("depth") * lev
    wet = level_ids < count[None, None, :]
    zero = jnp.zeros((), bf16)
    return jnp.where(wet, first, zero), jnp.where(wet, second, zero), grad[0]


def solution(mesh):
    return jax.shard_map(
        functools.partial(per_device, mesh.shape["horiz"], mesh.shape["depth"]),
        mesh=mesh,
        in_specs=(
            P(None, "depth", "horiz"),
            P("depth", "horiz", None, None, None),
            P("horiz", None),
            P(None, None, ("horiz", "depth")),
            P("depth", "horiz"),
            P(),
            P(None, "depth", "horiz"),
            P("horiz"),
        ),
        out_specs=(P(None, "depth", "horiz"), P(None, "depth", "horiz"), P()),
        check_vma=False,
    )
```
